256 devices in a mesh: grp: 8 (over x_hi, y), freq: 32 (over x_lo, z, core).
Axes of the slice: x: 4 (x_hi: 2, x_lo: 2; x = x_hi * 2 + x_lo), y: 4, z: 8, core: 2. Of those that a mesh axis runs over, the one named last changes fastest.
Arguments:
- transfer: bfloat16 [512, 2, 1024, 512], P('freq', None, 'grp'), may hold values from -0.1875 to 0.1875
- adjoint: bfloat16 [512, 2, 512, 128], P('freq'), may hold values from -6 to 6
- lower_rows: bfloat16 [1048576, 384], P(('grp', 'freq')), may hold values from -6 to 6
- pivot_store: bfloat16 [1024, 384], P('grp'), may hold values from -0.3125 to 0.3125
- owners: int32 [3], replicated, may hold values from 0 to 7
- inverse_factor: bfloat16 [128, 128], replicated, as said below
Outputs:
- panel: bfloat16 [1048576, 128], P(('grp', 'freq'))
The draws below stay inside these ranges and needn't reach their ends.
Inputs may be any that keep to these rules, and one draw needn't show every extreme that they name: `inverse_factor`: upper triangular, with diagonal entries from 0.5 to 2.
All inputs are finite; a program needn't handle non-finite values.
Results may differ from the reference program's by a relative error of at most 0.0059.
Values may be sent and summed in bfloat16 or wider, within the bound.
No kernel may reach another device: no remote copies, remote signals or barrier semaphores. Data moves between devices by JAX's collectives and lax.ppermute only.
A program may use at most 64 MiB of HBM per device.

```python
import math
import jax
import jax.numpy as jnp
from jax import lax

C = 128
M = 512
NF = 512
PANELS = 3
NT = 1024
NS = 1024
N_GRP = 8


def draw_inverse_factor(key, part):
    key = jax.random.fold_in(key, 7)
    diag_key, upper_key = jax.random.split(key)
    diagonal = jnp.exp(jax.random.uniform(diag_key, (C,), jnp.float32, math.log(0.5), math.log(2.0)))
    upper_part = 0.5 * jax.random.normal(upper_key, (C, C), jnp.float32) / math.sqrt(C)
    return (jnp.triu(upper_part, 1) + jnp.diag(diagonal)).astype(jnp.bfloat16)


def block_levels(own_key, dims, pieces, least, high):
    loudness = 1.0
    for dim, shards_of in pieces:
        heights = jax.random.uniform(jax.random.fold_in(jax.random.fold_in(own_key, 6), dim), (shards_of,), jnp.float32, least / len(pieces), high / len(pieces))
        loudness = loudness * jnp.repeat(jnp.exp(heights), dims[dim] // shards_of).reshape((-1,) + (1,) * (len(dims) - 1 - dim))
    return loudness


def centred(own_key, shape, width, bound, cuts=(), kind=jnp.bfloat16):
    gain = block_levels(own_key, shape, cuts, -0.22, 0.18) if cuts else 1.0
    entries = jax.random.normal(own_key, shape, jnp.float32) * width * gain
    return jnp.minimum(jnp.maximum(entries, -bound), bound).astype(kind)


def setup_inputs(seed: int = 0) -> dict:
    key_list = jax.random.split(jax.random.key(seed), 7)
    transfer = centred(key_list[0], (NF, 2, NS, M), (2 * M) ** -0.5, 0.1875, ((0, 32), (2, 8)))
    adjoint = centred(key_list[1], (NF, 2, M, C), 1.0, 6.0, ((0, 32),))
    lower_rows = centred(key_list[2], (NS * NT, PANELS * C), 1.0, 6.0, ((0, 256),))
    pivot_store = centred(key_list[3], (C * N_GRP, PANELS * C), (PANELS * C) ** -0.5, 0.3125, ((0, 8),))
    owners = jax.random.randint(key_list[4], (PANELS,), 0, N_GRP).astype(jnp.int32)
    inverse_factor = draw_inverse_factor(jax.random.fold_in(key_list[6], 71), 0)
    return dict(transfer=transfer, adjoint=adjoint, lower_rows=lower_rows, pivot_store=pivot_store, owners=owners, inverse_factor=inverse_factor)


def make_table(samples, frequencies):
    time_steps = jnp.arange(samples, dtype=jnp.int32)[:, None]
    wave_numbers = jnp.arange(frequencies, dtype=jnp.int32)[None, :]
    phases = (time_steps * wave_numbers % samples).astype(jnp.float32) * (2.0 * math.pi / samples)
    factor = 1.0 / math.sqrt(frequencies)
    return jnp.stack([jnp.cos(phases) * factor, -jnp.sin(phases) * factor]).astype(jnp.bfloat16)

def spectrum(operands):
    trans_pair, adjoint_pair = operands
    trans_pair = trans_pair.astype(jnp.float32)
    adjoint_pair = adjoint_pair.astype(jnp.float32)
    highest = lax.Precision.HIGHEST
    real_part = jnp.dot(trans_pair[0], adjoint_pair[0], precision=highest) - jnp.dot(trans_pair[1], adjoint_pair[1], precision=highest)
    imag_part = jnp.dot(trans_pair[0], adjoint_pair[1], precision=highest) + jnp.dot(trans_pair[1], adjoint_pair[0], precision=highest)
    return jnp.stack([real_part, imag_part], axis=1).astype(jnp.bfloat16)

def reference(transfer, adjoint, lower_rows, pivot_store, owners, inverse_factor):
    spectra = lax.map(spectrum, (transfer, adjoint))
    table = make_table(NT, NF)
    hessian = jnp.einsum('qtk,ksqc->stc', table.astype(jnp.float32), spectra.astype(jnp.float32), precision=lax.Precision.HIGHEST)
    hessian = hessian.reshape(NS * NT, C)
    blocks = []
    for panel_index in range(PANELS):
        row_start = (owners[panel_index] * C).astype(jnp.int32)
        col_start = jnp.asarray(panel_index * C).astype(jnp.int32)
        blocks.append(lax.dynamic_slice(pivot_store, (row_start, col_start), (C, C)))
    pivots = jnp.concatenate(blocks, axis=1)
    update = lax.dot_general(lower_rows, pivots, (((1,), (1,)), ((), ())), preferred_element_type=jnp.float32)
    reduced = (hessian - update).astype(jnp.bfloat16)
    return jnp.dot(reduced, inverse_factor, preferred_element_type=jnp.float32).astype(jnp.bfloat16)
```

```python
import math

import jax
import jax.numpy as jnp
import numpy as np
from jax import lax
from jax.experimental import pallas as pl
from jax.experimental.pallas import tpu as pltpu
from jax.sharding import PartitionSpec as P

C = 128
M = 512
NF = 512
PANELS = 3
NT = 1024
NS = 1024
N_GRP = 8
N_FREQ = 32
KL = NF // N_FREQ
SL = NS // N_GRP
SD = SL // N_FREQ
K_STEP = 4
T_STEP = 256


def table_columns():
    phases = np.arange(NT)[:, None] * np.arange(NF)[None, :] % NT * (2.0 * math.pi / NT)
    table = np.stack([np.cos(phases), -np.sin(phases)], axis=1) / math.sqrt(NF)
    table = table.reshape(NT, 2, N_FREQ, KL).transpose(0, 2, 1, 3).reshape(NT, 2 * NF)
    return table.astype(jnp.bfloat16)


def spectra_kernel(transfer_ref, adjoint_ref, out_ref, rows_ref):
    step = pl.program_id(0)
    for j in range(K_STEP):
        left = transfer_ref[j].reshape(2 * SL, M)
        right = jnp.concatenate([adjoint_ref[j, 0], adjoint_ref[j, 1]], axis=1)
        full = jnp.dot(left, right, preferred_element_type=jnp.float32)
        k = step * K_STEP + j
        rows_ref[pl.ds(k, SL, stride=2 * KL), :] = full[:SL, :C] - full[SL:, C:]
        rows_ref[pl.ds(KL + k, SL, stride=2 * KL), :] = full[:SL, C:] + full[SL:, :C]

    @pl.when(step == KL // K_STEP - 1)
    def _():
        out_ref[...] = rows_ref[...].astype(jnp.bfloat16)


def spectra_rows(transfer, adjoint):
    return pl.pallas_call(
        spectra_kernel,
        grid=(KL // K_STEP,),
        in_specs=[
            pl.BlockSpec((K_STEP, 2, SL, M), lambda i: (i, 0, 0, 0)),
            pl.BlockSpec((K_STEP, 2, M, C), lambda i: (i, 0, 0, 0)),
        ],
        out_specs=pl.BlockSpec((SL * 2 * KL, C), lambda i: (0, 0)),
        out_shape=jax.ShapeDtypeStruct((SL * 2 * KL, C), jnp.bfloat16),
        scratch_shapes=[pltpu.VMEM((SL * 2 * KL, C), jnp.float32)],
        compiler_params=pltpu.CompilerParams(vmem_limit_bytes=32 * 2**20),
        name="spectra",
    )(transfer, adjoint)


def panel_kernel(table_ref, recv_ref, lower_ref, pivots_ref, inverse_ref, out_ref):
    table = table_ref[...]
    pivots = pivots_ref[...]
    inverse = inverse_ref[...]
    for pair in range(SD // 2):
        cols = [recv_ref[:, 2 * pair + i].reshape(2 * NF, C) for i in range(2)]
        both = jnp.dot(table, jnp.concatenate(cols, axis=1), preferred_element_type=jnp.float32)
        for i in range(2):
            s = 2 * pair + i
            update = lax.dot_general(
                lower_ref[s], pivots, (((1,), (1,)), ((), ())), preferred_element_type=jnp.float32
            )
            reduced = (both[:, i * C : (i + 1) * C] - update).astype(jnp.bfloat16)
            out_ref[s] = jnp.dot(reduced, inverse, preferred_element_type=jnp.float32).astype(jnp.bfloat16)


def panel_rows(table, recv, lower, pivots, inverse):
    return pl.pallas_call(
        panel_kernel,
        grid=(NT // T_STEP,),
        in_specs=[
            pl.BlockSpec((T_STEP, 2 * NF), lambda i: (i, 0)),
            pl.BlockSpec((N_FREQ, SD, 2 * KL, C), lambda i: (0, 0, 0, 0)),
            pl.BlockSpec((SD, T_STEP, PANELS * C), lambda i: (0, i, 0)),
            pl.BlockSpec((C, PANELS * C), lambda i: (0, 0)),
            pl.BlockSpec((C, C), lambda i: (0, 0)),
        ],
        out_specs=pl.BlockSpec((SD, T_STEP, C), lambda i: (0, i, 0)),
        out_shape=jax.ShapeDtypeStruct((SD, NT, C), jnp.bfloat16),
        compiler_params=pltpu.CompilerParams(vmem_limit_bytes=32 * 2**20),
        name="panel",
    )(table, recv, lower, pivots, inverse)


def gather_pivots(pivot_store, owners):
    mine = jnp.repeat(owners == lax.axis_index("grp"), C)[None, :]
    value = jnp.where(mine, pivot_store, jnp.zeros_like(pivot_store))
    for bit in (1, 2, 4):
        value = value + lax.ppermute(value, "grp", [(g, g ^ bit) for g in range(N_GRP)])
    return value


def per_device(transfer, adjoint, lower_rows, pivot_store, owners, inverse_factor):
    rows = spectra_rows(transfer, adjoint)
    recv = lax.all_to_all(rows.reshape(N_FREQ, SD, 2 * KL, C), "freq", split_axis=0, concat_axis=0, tiled=True)
    pivots = gather_pivots(pivot_store, owners)
    table = jnp.asarray(table_columns())
    out = panel_rows(table, recv, lower_rows.reshape(SD, NT, PANELS * C), pivots, inverse_factor)
    return out.reshape(SD * NT, C)


def solution(mesh):
    in_specs = (
        P("freq", None, "grp", None),
        P("freq", None, None, None),
        P(("grp", "freq"), None),
        P("grp", None),
        P(),
        P(),
    )
    out_specs = P(("grp", "freq"), None)
    return jax.shard_map(
        per_device, mesh=mesh, in_specs=in_specs, out_specs=out_specs, check_vma=False
    )
```

```python
import math

import jax
import jax.numpy as jnp
import numpy as np
from jax import lax
from jax.experimental import pallas as pl
from jax.experimental.pallas import tpu as pltpu
from jax.sharding import PartitionSpec as P

C = 128
M = 512
NF = 512
PANELS = 3
NT = 1024
NS = 1024
N_GRP = 8
N_FREQ = 32
KL = NF // N_FREQ
SL = NS // N_GRP
SD = SL // N_FREQ
ROWS = 2 * KL
PITCH = ROWS + 1
CHUNKS = 8
HALF = NT // 2
T_CHUNK = 128


def table_halves():
    phases = np.arange(HALF)[:, None] * np.arange(NF)[None, :] % NT * (2.0 * math.pi / NT)
    table = np.stack([np.cos(phases), -np.sin(phases)], axis=1) / math.sqrt(NF)
    table = table.reshape(HALF, 2, N_FREQ, KL // 2, 2).transpose(4, 0, 2, 1, 3).reshape(2, HALF, NF)
    return table.astype(jnp.bfloat16)


def spectra_kernel(transfer_hbm, adjoint_hbm, out_ref, transfer_ref, adjoint_ref, rows_ref, sems):
    per = KL // CHUNKS
    copies = []
    for i in range(CHUNKS):
        part = pl.ds(i * per, per)
        for j, (src, dst) in enumerate(((transfer_hbm, transfer_ref), (adjoint_hbm, adjoint_ref))):
            copy = pltpu.make_async_copy(src.at[part], dst.at[part], sems.at[j, i])
            copy.start()
            copies.append(copy)
    for k in range(KL):
        if k % per == 0:
            copies[k // per * 2].wait()
            copies[k // per * 2 + 1].wait()
        left = transfer_ref[k].reshape(2 * SL, M)
        right = jnp.concatenate([adjoint_ref[k, 0], adjoint_ref[k, 1]], axis=1)
        full = jnp.dot(left, right, preferred_element_type=jnp.float32)
        row = k % 2 * KL + k // 2
        rows_ref[pl.ds(row, SL, stride=PITCH), :] = full[:SL, :C] - full[SL:, C:]
        rows_ref[pl.ds(row + KL // 2, SL, stride=PITCH), :] = full[:SL, C:] + full[SL:, :C]
    for s in range(SL):
        out_ref[pl.ds(s * ROWS, ROWS), :] = rows_ref[pl.ds(s * PITCH, ROWS), :].astype(jnp.bfloat16)


def spectra_rows(transfer, adjoint):
    return pl.pallas_call(
        spectra_kernel,
        in_specs=[pl.BlockSpec(memory_space=pl.ANY)] * 2,
        out_specs=pl.BlockSpec(memory_space=pltpu.VMEM),
        out_shape=jax.ShapeDtypeStruct((SL * ROWS, C), jnp.bfloat16),
        scratch_shapes=[
            pltpu.VMEM((KL, 2, SL, M), jnp.bfloat16),
            pltpu.VMEM((KL, 2, M, C), jnp.bfloat16),
            pltpu.VMEM((SL * PITCH + PITCH + 7, C), jnp.float32),
            pltpu.SemaphoreType.DMA((2, CHUNKS)),
        ],
        compiler_params=pltpu.CompilerParams(vmem_limit_bytes=60 * 2**20),
        name="spectra",
    )(transfer, adjoint)


def update_kernel(lower_ref, pivots_ref, out_ref):
    out_ref[...] = lax.dot_general(
        lower_ref[...], pivots_ref[...], (((1,), (1,)), ((), ())), preferred_element_type=jnp.float32
    )


def update_rows(lower, pivots):
    rows = lower.shape[0]
    step = rows // 4
    return pl.pallas_call(
        update_kernel,
        grid=(rows // step,),
        in_specs=[
            pl.BlockSpec((step, PANELS * C), lambda i: (i, 0)),
            pl.BlockSpec((C, PANELS * C), lambda i: (0, 0)),
        ],
        out_specs=pl.BlockSpec((step, C), lambda i: (i, 0)),
        out_shape=jax.ShapeDtypeStruct((rows, C), jnp.float32),
        compiler_params=pltpu.CompilerParams(vmem_limit_bytes=16 * 2**20),
        cost_estimate=pl.CostEstimate(
            flops=2 * rows * PANELS * C * C, bytes_accessed=rows * (PANELS * C * 2 + C * 4), transcendentals=0
        ),
        name="update",
    )(lower, pivots)


def panel_kernel(table_ref, recv_ref, update_ref, inverse_ref, out_hbm, out_ref, sems):
    inverse = inverse_ref[...]
    sides = []
    for parity in range(2):
        cols = [recv_ref[:, s, parity].reshape(NF, C) for s in range(SD)]
        sides.append(jnp.concatenate(cols, axis=1))
    copies = []
    for i in range(HALF // T_CHUNK):
        part = pl.ds(i * T_CHUNK, T_CHUNK)
        even = jnp.dot(table_ref[0, part], sides[0], preferred_element_type=jnp.float32)
        odd = jnp.dot(table_ref[1, part], sides[1], preferred_element_type=jnp.float32)
        for half, sums in enumerate((even + odd, even - odd)):
            where = pl.ds(half * HALF + i * T_CHUNK, T_CHUNK)
            for s in range(SD):
                reduced = (sums[:, s * C : (s + 1) * C] - update_ref[s, where]).astype(jnp.bfloat16)
                out_ref[s, where] = jnp.dot(reduced, inverse, preferred_element_type=jnp.float32).astype(jnp.bfloat16)
            copy = pltpu.make_async_copy(out_ref.at[:, where], out_hbm.at[:, where], sems.at[2 * i + half])
            copy.start()
            copies.append(copy)
    for copy in copies:
        copy.wait()


def panel_rows(table, recv, update, inverse):
    return pl.pallas_call(
        panel_kernel,
        in_specs=[pl.BlockSpec(memory_space=pltpu.VMEM)] * 4,
        out_specs=pl.BlockSpec(memory_space=pl.ANY),
        out_shape=jax.ShapeDtypeStruct((SD, NT, C), jnp.bfloat16),
        scratch_shapes=[
            pltpu.VMEM((SD, NT, C), jnp.bfloat16),
            pltpu.SemaphoreType.DMA((2 * HALF // T_CHUNK,)),
        ],
        compiler_params=pltpu.CompilerParams(vmem_limit_bytes=24 * 2**20),
        name="panel",
    )(table, recv, update, inverse)


def gather_pivots(pivot_store, owners):
    mine = jnp.repeat(owners == lax.axis_index("grp"), C)[None, :]
    value = jnp.where(mine, pivot_store, jnp.zeros_like(pivot_store))
    for bit in (1, 2, 4):
        value = value + lax.ppermute(value, "grp", [(g, g ^ bit) for g in range(N_GRP)])
    return value


def per_device(transfer, adjoint, lower_rows, pivot_store, owners, inverse_factor):
    rows = spectra_rows(transfer, adjoint)
    recv = lax.all_to_all(rows.reshape(N_FREQ, SD, 2, KL, C), "freq", split_axis=0, concat_axis=0, tiled=True)
    pivots = gather_pivots(pivot_store, owners)
    update = update_rows(lower_rows, pivots)
    table = jnp.asarray(table_halves())
    out = panel_rows(table, recv, update.reshape(SD, NT, C), inverse_factor)
    return out.reshape(SD * NT, C)


def solution(mesh):
    in_specs = (
        P("freq", None, "grp", None),
        P("freq", None, None, None),
        P(("grp", "freq"), None),
        P("grp", None),
        P(),
        P(),
    )
    out_specs = P(("grp", "freq"), None)
    return jax.shard_map(
        per_device, mesh=mesh, in_specs=in_specs, out_specs=out_specs, check_vma=False
    )
```

```python
import math

import jax
import jax.numpy as jnp
import numpy as np
from jax import lax
from jax.experimental import pallas as pl
from jax.experimental.pallas import tpu as pltpu
from jax.sharding import PartitionSpec as P

C = 128
M = 512
NF = 512
PANELS = 3
NT = 1024
NS = 1024
N_GRP = 8
N_FREQ = 32
KL = NF // N_FREQ
SL = NS // N_GRP
SD = SL // N_FREQ
ROWS = 2 * KL
PITCH = ROWS + 1
LOADS = 4
HALF = NT // 2
T_STEP = HALF // 2
T_CHUNK = 128


def table_parts():
    phases = np.arange(HALF)[:, None] * np.arange(NF)[None, :] % NT * (2.0 * math.pi / NT)
    table = np.stack([np.cos(phases), -np.sin(phases)], axis=1) / math.sqrt(NF)
    table = table.reshape(HALF, 2, N_FREQ, KL // 2, 2).transpose(4, 0, 2, 1, 3).reshape(2, HALF, NF)
    return np.concatenate([table[0, : HALF // 2], table[1]]).astype(jnp.bfloat16)


def spectra_kernel(
    transfer_hbm, adjoint_hbm, out_hbm, transfer_ref, adjoint_ref, rows_ref, out_ref, load_sems, out_sems
):
    per = KL // 2 // LOADS
    loads = []
    for parity in range(2):
        for i in range(LOADS):
            part = pl.ds(i * per, per)
            for j, (src, dst) in enumerate(((transfer_hbm, transfer_ref), (adjoint_hbm, adjoint_ref))):
                copy = pltpu.make_async_copy(src.at[part, parity], dst.at[parity, part], load_sems.at[j, parity, i])
                copy.start()
                loads.append(copy)
    stores = []
    for parity in range(2):
        for k in range(KL // 2):
            if k % per == 0:
                first = 2 * (parity * LOADS + k // per)
                loads[first].wait()
                loads[first + 1].wait()
            left = transfer_ref[parity, k].reshape(2 * SL, M)
            right = jnp.concatenate([adjoint_ref[parity, k, 0], adjoint_ref[parity, k, 1]], axis=1)
            full = jnp.dot(left, right, preferred_element_type=jnp.float32)
            row = parity * KL + k
            rows_ref[pl.ds(row, SL, stride=PITCH), :] = full[:SL, :C] - full[SL:, C:]
            rows_ref[pl.ds(row + KL // 2, SL, stride=PITCH), :] = full[:SL, C:] + full[SL:, :C]
        for s in range(SL):
            out_ref[s, parity] = rows_ref[pl.ds(s * PITCH + parity * KL, KL), :].astype(jnp.bfloat16)
        copy = pltpu.make_async_copy(out_ref.at[:, parity], out_hbm.at[:, parity], out_sems.at[parity])
        copy.start()
        stores.append(copy)
    for copy in stores:
        copy.wait()


def spectra_rows(transfer, adjoint):
    return pl.pallas_call(
        spectra_kernel,
        in_specs=[pl.BlockSpec(memory_space=pl.ANY)] * 2,
        out_specs=pl.BlockSpec(memory_space=pl.ANY),
        out_shape=jax.ShapeDtypeStruct((SL, 2, KL, C), jnp.bfloat16),
        scratch_shapes=[
            pltpu.VMEM((2, KL // 2, 2, SL, M), jnp.bfloat16),
            pltpu.VMEM((2, KL // 2, 2, M, C), jnp.bfloat16),
            pltpu.VMEM((SL * PITCH + PITCH + 7, C), jnp.float32),
            pltpu.VMEM((SL, 2, KL, C), jnp.bfloat16),
            pltpu.SemaphoreType.DMA((2, 2, LOADS)),
            pltpu.SemaphoreType.DMA((2,)),
        ],
        compiler_params=pltpu.CompilerParams(vmem_limit_bytes=60 * 2**20),
        name="spectra",
    )(transfer.reshape(KL // 2, 2, 2, SL, M), adjoint.reshape(KL // 2, 2, 2, M, C))


def update_kernel(lower_ref, pivots_ref, high_ref, low_ref):
    update = lax.dot_general(
        lower_ref[...], pivots_ref[...], (((1,), (1,)), ((), ())), preferred_element_type=jnp.float32
    )
    high = update.astype(jnp.bfloat16)
    high_ref[...] = high
    low_ref[...] = (update - high.astype(jnp.float32)).astype(low_ref.dtype)


def update_rows(lower, pivots):
    rows = lower.shape[0]
    return pl.pallas_call(
        update_kernel,
        in_specs=[pl.BlockSpec(memory_space=pltpu.VMEM)] * 2,
        out_specs=[pl.BlockSpec(memory_space=pltpu.VMEM)] * 2,
        out_shape=[
            jax.ShapeDtypeStruct((rows, C), jnp.bfloat16),
            jax.ShapeDtypeStruct((rows, C), jnp.float8_e5m2),
        ],
        compiler_params=pltpu.CompilerParams(vmem_limit_bytes=24 * 2**20),
        cost_estimate=pl.CostEstimate(
            flops=2 * rows * PANELS * C * C, bytes_accessed=rows * (PANELS * C * 2 + C * 3), transcendentals=0
        ),
        name="update",
    )(lower, pivots)


def panel_kernel(
    table_ref, recv_ref, high_ref, low_ref, inverse_hbm, out_hbm, out_ref, inverse_ref, block_ref, sems, sem
):
    load = pltpu.make_async_copy(inverse_hbm, inverse_ref, sem)
    load.start()
    block_ref[...] = jnp.zeros_like(block_ref)
    sides = []
    for parity in range(2):
        cols = [recv_ref[:, s, parity].reshape(NF, C) for s in range(SD)]
        sides.append(jnp.concatenate(cols, axis=1))
    stores = []
    for first in range(0, HALF, T_STEP):
        rows = table_ref[pl.ds(0, T_STEP)]
        if first > 0:
            column = lax.broadcasted_iota(jnp.int32, rows.shape, 1)
            rows = jnp.where(column % 2 == 0, rows.astype(jnp.float32), -rows.astype(jnp.float32)).astype(jnp.bfloat16)
        even = jnp.dot(rows, sides[0], preferred_element_type=jnp.float32)
        rows = table_ref[pl.ds(T_STEP + first, T_STEP)]
        odd = jnp.dot(rows, sides[1], preferred_element_type=jnp.float32)
        if first == 0:
            load.wait()
            block_ref[:C, :C] = inverse_ref[...]
            block_ref[C:, C:] = inverse_ref[...]
            block = block_ref[...]
        for i in range(0, T_STEP, T_CHUNK):
            chunk = slice(i, i + T_CHUNK)
            for half, sums in enumerate((even[chunk] + odd[chunk], even[chunk] - odd[chunk])):
                where = pl.ds(half * HALF + first + i, T_CHUNK)
                for s in range(0, SD, 2):
                    update = [
                        high_ref[j, where].astype(jnp.float32) + low_ref[j, where].astype(jnp.float32)
                        for j in (s, s + 1)
                    ]
                    update = jnp.concatenate(update, axis=1)
                    reduced = (sums[:, s * C : (s + 2) * C] - update).astype(jnp.bfloat16)
                    both = jnp.dot(reduced, block, preferred_element_type=jnp.float32).astype(jnp.bfloat16)
                    out_ref[s, where] = both[:, :C]
                    out_ref[s + 1, where] = both[:, C:]
                copy = pltpu.make_async_copy(out_ref.at[:, where], out_hbm.at[:, where], sems.at[len(stores)])
                copy.start()
                stores.append(copy)
    for copy in stores:
        copy.wait()


def panel_rows(table, recv, high, low, inverse):
    return pl.pallas_call(
        panel_kernel,
        in_specs=[pl.BlockSpec(memory_space=pltpu.VMEM)] * 4 + [pl.BlockSpec(memory_space=pl.ANY)],
        out_specs=pl.BlockSpec(memory_space=pl.ANY),
        out_shape=jax.ShapeDtypeStruct((SD, NT, C), jnp.bfloat16),
        scratch_shapes=[
            pltpu.VMEM((SD, NT, C), jnp.bfloat16),
            pltpu.VMEM((C, C), jnp.bfloat16),
            pltpu.VMEM((2 * C, 2 * C), jnp.bfloat16),
            pltpu.SemaphoreType.DMA((NT // T_CHUNK,)),
            pltpu.SemaphoreType.DMA,
        ],
        compiler_params=pltpu.CompilerParams(vmem_limit_bytes=24 * 2**20),
        name="panel",
    )(table, recv, high, low, inverse)


def gather_pivots(pivot_store, owners):
    mine = jnp.repeat(owners == lax.axis_index("grp"), C)[None, :]
    value = jnp.where(mine, pivot_store, jnp.zeros_like(pivot_store))
    for bit in (1, 2, 4):
        value = value + lax.ppermute(value, "grp", [(g, g ^ bit) for g in range(N_GRP)])
    return value


def per_device(transfer, adjoint, lower_rows, pivot_store, owners, inverse_factor):
    rows = spectra_rows(transfer, adjoint)
    recv = lax.all_to_all(rows.reshape(N_FREQ, SD, 2, KL, C), "freq", split_axis=0, concat_axis=0, tiled=True)
    pivots = gather_pivots(pivot_store, owners)
    high, low = update_rows(lower_rows, pivots)
    out = panel_rows(jnp.asarray(table_parts()), recv, high.reshape(SD, NT, C), low.reshape(SD, NT, C), inverse_factor)
    return out.reshape(SD * NT, C)


def solution(mesh):
    in_specs = (
        P("freq", None, "grp", None),
        P("freq", None, None, None),
        P(("grp", "freq"), None),
        P("grp", None),
        P(),
        P(),
    )
    out_specs = P(("grp", "freq"), None)
    return jax.shard_map(
        per_device, mesh=mesh, in_specs=in_specs, out_specs=out_specs, check_vma=False
    )
```

```python
import math

import jax
import jax.numpy as jnp
import numpy as np
from jax import lax
from jax.experimental import pallas as pl
from jax.experimental.pallas import tpu as pltpu
from jax.sharding import PartitionSpec as P

C = 128
M = 512
NF = 512
PANELS = 3
NT = 1024
NS = 1024
N_GRP = 8
N_FREQ = 32
KL = NF // N_FREQ
SL = NS // N_GRP
SD = SL // N_FREQ
ORDER = [x * 16 + (z + 5) % 8 * 2 + core for x in range(2) for z in range(8) for core in range(2)]
ROWS = 2 * KL
PITCH = ROWS + 1
LOADS = 4
HALF = NT // 2
T_STEP = HALF // 2
T_CHUNK = 128


def table_parts():
    phases = np.arange(HALF)[:, None] * np.arange(NF)[None, :] % NT * (2.0 * math.pi / NT)
    table = np.stack([np.cos(phases), -np.sin(phases)], axis=1) / math.sqrt(NF)
    table = table.reshape(HALF, 2, N_FREQ, KL // 2, 2)[:, :, ORDER].transpose(4, 0, 2, 1, 3).reshape(2, HALF, NF)
    return np.concatenate([table[0, : HALF // 2], table[1]]).astype(jnp.bfloat16)


def spectra_kernel(
    transfer_hbm, adjoint_hbm, out_hbm, transfer_ref, adjoint_ref, rows_ref, out_ref, load_sems, out_sems
):
    per = KL // 2 // LOADS
    loads = []
    for parity in range(2):
        for i in range(LOADS):
            part = pl.ds(i * per, per)
            for j, (src, dst) in enumerate(((transfer_hbm, transfer_ref), (adjoint_hbm, adjoint_ref))):
                copy = pltpu.make_async_copy(src.at[part, parity], dst.at[parity, part], load_sems.at[j, parity, i])
                copy.start()
                loads.append(copy)
    stores = []
    for parity in range(2):
        for k in range(KL // 2):
            if k % per == 0:
                first = 2 * (parity * LOADS + k // per)
                loads[first].wait()
                loads[first + 1].wait()
            left = transfer_ref[parity, k].reshape(2 * SL, M)
            right = jnp.concatenate([adjoint_ref[parity, k, 0], adjoint_ref[parity, k, 1]], axis=1)
            full = jnp.dot(left, right, preferred_element_type=jnp.float32)
            row = parity * KL + k
            rows_ref[pl.ds(row, SL, stride=PITCH), :] = full[:SL, :C] - full[SL:, C:]
            rows_ref[pl.ds(row + KL // 2, SL, stride=PITCH), :] = full[:SL, C:] + full[SL:, :C]
        for s in range(SL):
            place = ORDER.index(s // SD) * SD + s % SD
            out_ref[place, parity] = rows_ref[pl.ds(s * PITCH + parity * KL, KL), :].astype(jnp.bfloat16)
        copy = pltpu.make_async_copy(out_ref.at[:, parity], out_hbm.at[:, parity], out_sems.at[parity])
        copy.start()
        stores.append(copy)
    for copy in stores:
        copy.wait()


def spectra_rows(transfer, adjoint):
    return pl.pallas_call(
        spectra_kernel,
        in_specs=[pl.BlockSpec(memory_space=pl.ANY)] * 2,
        out_specs=pl.BlockSpec(memory_space=pl.ANY),
        out_shape=jax.ShapeDtypeStruct((SL, 2, KL, C), jnp.bfloat16),
        scratch_shapes=[
            pltpu.VMEM((2, KL // 2, 2, SL, M), jnp.bfloat16),
            pltpu.VMEM((2, KL // 2, 2, M, C), jnp.bfloat16),
            pltpu.VMEM((SL * PITCH + PITCH + 7, C), jnp.float32),
            pltpu.VMEM((SL, 2, KL, C), jnp.bfloat16),
            pltpu.SemaphoreType.DMA((2, 2, LOADS)),
            pltpu.SemaphoreType.DMA((2,)),
        ],
        compiler_params=pltpu.CompilerParams(vmem_limit_bytes=60 * 2**20),
        name="spectra",
    )(transfer.reshape(KL // 2, 2, 2, SL, M), adjoint.reshape(KL // 2, 2, 2, M, C))


def update_kernel(lower_ref, pivots_ref, high_ref, low_ref):
    update = lax.dot_general(
        lower_ref[...], pivots_ref[...], (((1,), (1,)), ((), ())), preferred_element_type=jnp.float32
    )
    high = update.astype(jnp.bfloat16)
    high_ref[...] = high
    low_ref[...] = (update - high.astype(jnp.float32)).astype(low_ref.dtype)


def update_rows(lower, pivots):
    rows = lower.shape[0]
    return pl.pallas_call(
        update_kernel,
        in_specs=[pl.BlockSpec(memory_space=pltpu.VMEM)] * 2,
        out_specs=[pl.BlockSpec(memory_space=pltpu.VMEM)] * 2,
        out_shape=[
            jax.ShapeDtypeStruct((rows, C), jnp.bfloat16),
            jax.ShapeDtypeStruct((rows, C), jnp.float8_e5m2),
        ],
        compiler_params=pltpu.CompilerParams(vmem_limit_bytes=24 * 2**20),
        cost_estimate=pl.CostEstimate(
            flops=2 * rows * PANELS * C * C, bytes_accessed=rows * (PANELS * C * 2 + C * 3), transcendentals=0
        ),
        name="update",
    )(lower, pivots)


def panel_kernel(
    table_ref, recv_ref, high_ref, low_ref, inverse_hbm, out_hbm, out_ref, inverse_ref, block_ref, sems, sem
):
    load = pltpu.make_async_copy(inverse_hbm, inverse_ref, sem)
    load.start()
    block_ref[...] = jnp.zeros_like(block_ref)
    sides = []
    for parity in range(2):
        cols = [recv_ref[:, s, parity].reshape(NF, C) for s in range(SD)]
        sides.append(jnp.concatenate(cols, axis=1))
    stores = []
    for first in range(0, HALF, T_STEP):
        rows = table_ref[pl.ds(0, T_STEP)]
        if first > 0:
            column = lax.broadcasted_iota(jnp.int32, rows.shape, 1)
            rows = jnp.where(column % 2 == 0, rows.astype(jnp.float32), -rows.astype(jnp.float32)).astype(jnp.bfloat16)
        even = jnp.dot(rows, sides[0], preferred_element_type=jnp.float32)
        rows = table_ref[pl.ds(T_STEP + first, T_STEP)]
        odd = jnp.dot(rows, sides[1], preferred_element_type=jnp.float32)
        if first == 0:
            load.wait()
            block_ref[:C, :C] = inverse_ref[...]
            block_ref[C:, C:] = inverse_ref[...]
            block = block_ref[...]
        for i in range(0, T_STEP, T_CHUNK):
            chunk = slice(i, i + T_CHUNK)
            for half, sums in enumerate((even[chunk] + odd[chunk], even[chunk] - odd[chunk])):
                where = pl.ds(half * HALF + first + i, T_CHUNK)
                for s in range(0, SD, 2):
                    update = [
                        high_ref[j, where].astype(jnp.float32) + low_ref[j, where].astype(jnp.float32)
                        for j in (s, s + 1)
                    ]
                    update = jnp.concatenate(update, axis=1)
                    reduced = (sums[:, s * C : (s + 2) * C] - update).astype(jnp.bfloat16)
                    both = jnp.dot(reduced, block, preferred_element_type=jnp.float32).astype(jnp.bfloat16)
                    out_ref[s, where] = both[:, :C]
                    out_ref[s + 1, where] = both[:, C:]
                copy = pltpu.make_async_copy(out_ref.at[:, where], out_hbm.at[:, where], sems.at[len(stores)])
                copy.start()
                stores.append(copy)
    for copy in stores:
        copy.wait()


def panel_rows(table, recv, high, low, inverse):
    return pl.pallas_call(
        panel_kernel,
        in_specs=[pl.BlockSpec(memory_space=pltpu.VMEM)] * 4 + [pl.BlockSpec(memory_space=pl.ANY)],
        out_specs=pl.BlockSpec(memory_space=pl.ANY),
        out_shape=jax.ShapeDtypeStruct((SD, NT, C), jnp.bfloat16),
        scratch_shapes=[
            pltpu.VMEM((SD, NT, C), jnp.bfloat16),
            pltpu.VMEM((C, C), jnp.bfloat16),
            pltpu.VMEM((2 * C, 2 * C), jnp.bfloat16),
            pltpu.SemaphoreType.DMA((NT // T_CHUNK,)),
            pltpu.SemaphoreType.DMA,
        ],
        compiler_params=pltpu.CompilerParams(vmem_limit_bytes=24 * 2**20),
        name="panel",
    )(table, recv, high, low, inverse)


def gather_pivots(pivot_store, owners):
    mine = jnp.repeat(owners == lax.axis_index("grp"), C)[None, :]
    value = jnp.where(mine, pivot_store, jnp.zeros_like(pivot_store))
    for bit in (1, 2, 4):
        value = value + lax.ppermute(value, "grp", [(g, g ^ bit) for g in range(N_GRP)])
    return value


def per_device(transfer, adjoint, lower_rows, pivot_store, owners, inverse_factor):
    rows = spectra_rows(transfer, adjoint)
    rows = rows.reshape(N_FREQ, SD, 2, KL, C)
    recv = lax.all_to_all(rows, "freq", split_axis=0, concat_axis=0, axis_index_groups=[ORDER], tiled=True)
    pivots = gather_pivots(pivot_store, owners)
    high, low = update_rows(lower_rows, pivots)
    out = panel_rows(jnp.asarray(table_parts()), recv, high.reshape(SD, NT, C), low.reshape(SD, NT, C), inverse_factor)
    return out.reshape(SD * NT, C)


def solution(mesh):
    in_specs = (
        P("freq", None, "grp", None),
        P("freq", None, None, None),
        P(("grp", "freq"), None),
        P("grp", None),
        P(),
        P(),
    )
    out_specs = P(("grp", "freq"), None)
    return jax.shard_map(
        per_device, mesh=mesh, in_specs=in_specs, out_specs=out_specs, check_vma=False
    )
```

```python
import math

import jax
import jax.numpy as jnp
import numpy as np
from jax import lax
from jax.experimental import pallas as pl
from jax.experimental.pallas import tpu as pltpu
from jax.sharding import PartitionSpec as P

C = 128
M = 512
NF = 512
PANELS = 3
NT = 1024
NS = 1024
N_GRP = 8
N_FREQ = 32
KL = NF // N_FREQ
SL = NS // N_GRP
SD = SL // N_FREQ
ORDER = [x * 16 + (z + 5) % 8 * 2 + 1 - core for x in range(2) for z in range(8) for core in range(2)]
ROWS = 2 * KL
PITCH = ROWS + 1
LOADS = 4
HALF = NT // 2
T_STEP = HALF // 2
T_CHUNK = 128


def table_parts():
    phases = np.arange(HALF)[:, None] * np.arange(NF)[None, :] % NT * (2.0 * math.pi / NT)
    table = np.stack([np.cos(phases), -np.sin(phases)], axis=1) / math.sqrt(NF)
    table = table.reshape(HALF, 2, N_FREQ, KL // 2, 2)[:, :, ORDER].transpose(4, 0, 2, 1, 3).reshape(2, HALF, NF)
    return np.concatenate([table[0, : HALF // 2], table[1]]).astype(jnp.bfloat16)


def spectra_kernel(
    transfer_hbm, adjoint_hbm, out_hbm, transfer_ref, adjoint_ref, rows_ref, out_ref, load_sems, out_sems
):
    per = KL // 2 // LOADS
    loads = []
    for parity in range(2):
        for i in range(LOADS):
            part = pl.ds(i * per, per)
            for j, (src, dst) in enumerate(((transfer_hbm, transfer_ref), (adjoint_hbm, adjoint_ref))):
                copy = pltpu.make_async_copy(src.at[part, parity], dst.at[parity, part], load_sems.at[j, parity, i])
                copy.start()
                loads.append(copy)
    stores = []
    for parity in range(2):
        for k in range(KL // 2):
            if k % per == 0:
                first = 2 * (parity * LOADS + k // per)
                loads[first].wait()
                loads[first + 1].wait()
            left = transfer_ref[parity, k].reshape(2 * SL, M)
            right = jnp.concatenate([adjoint_ref[parity, k, 0], adjoint_ref[parity, k, 1]], axis=1)
            full = jnp.dot(left, right, preferred_element_type=jnp.float32)
            row = parity * KL + k
            rows_ref[pl.ds(row, SL, stride=PITCH), :] = full[:SL, :C] - full[SL:, C:]
            rows_ref[pl.ds(row + KL // 2, SL, stride=PITCH), :] = full[:SL, C:] + full[SL:, :C]
        for s in range(SL):
            place = ORDER.index(s // SD) * SD + s % SD
            out_ref[place, parity] = rows_ref[pl.ds(s * PITCH + parity * KL, KL), :].astype(jnp.bfloat16)
        copy = pltpu.make_async_copy(out_ref.at[:, parity], out_hbm.at[:, parity], out_sems.at[parity])
        copy.start()
        stores.append(copy)
    for copy in stores:
        copy.wait()


def spectra_rows(transfer, adjoint):
    return pl.pallas_call(
        spectra_kernel,
        in_specs=[pl.BlockSpec(memory_space=pl.ANY)] * 2,
        out_specs=pl.BlockSpec(memory_space=pl.ANY),
        out_shape=jax.ShapeDtypeStruct((SL, 2, KL, C), jnp.bfloat16),
        scratch_shapes=[
            pltpu.VMEM((2, KL // 2, 2, SL, M), jnp.bfloat16),
            pltpu.VMEM((2, KL // 2, 2, M, C), jnp.bfloat16),
            pltpu.VMEM((SL * PITCH + PITCH + 7, C), jnp.float32),
            pltpu.VMEM((SL, 2, KL, C), jnp.bfloat16),
            pltpu.SemaphoreType.DMA((2, 2, LOADS)),
            pltpu.SemaphoreType.DMA((2,)),
        ],
        compiler_params=pltpu.CompilerParams(vmem_limit_bytes=60 * 2**20),
        name="spectra",
    )(transfer.reshape(KL // 2, 2, 2, SL, M), adjoint.reshape(KL // 2, 2, 2, M, C))


def update_kernel(lower_ref, pivots_ref, high_ref, low_ref):
    update = lax.dot_general(
        lower_ref[...], pivots_ref[...], (((1,), (1,)), ((), ())), preferred_element_type=jnp.float32
    )
    high = update.astype(jnp.bfloat16)
    high_ref[...] = high
    low_ref[...] = (update - high.astype(jnp.float32)).astype(low_ref.dtype)


def update_rows(lower, pivots):
    rows = lower.shape[0]
    return pl.pallas_call(
        update_kernel,
        in_specs=[pl.BlockSpec(memory_space=pltpu.VMEM)] * 2,
        out_specs=[pl.BlockSpec(memory_space=pltpu.VMEM)] * 2,
        out_shape=[
            jax.ShapeDtypeStruct((rows, C), jnp.bfloat16),
            jax.ShapeDtypeStruct((rows, C), jnp.float8_e5m2),
        ],
        compiler_params=pltpu.CompilerParams(vmem_limit_bytes=24 * 2**20),
        cost_estimate=pl.CostEstimate(
            flops=2 * rows * PANELS * C * C, bytes_accessed=rows * (PANELS * C * 2 + C * 3), transcendentals=0
        ),
        name="update",
    )(lower, pivots)


def panel_kernel(
    table_ref, recv_ref, high_ref, low_ref, inverse_hbm, out_hbm, out_ref, inverse_ref, block_ref, sems, sem
):
    load = pltpu.make_async_copy(inverse_hbm, inverse_ref, sem)
    load.start()
    block_ref[...] = jnp.zeros_like(block_ref)
    sides = []
    for parity in range(2):
        cols = [recv_ref[:, s, parity].reshape(NF, C) for s in range(SD)]
        sides.append(jnp.concatenate(cols, axis=1))
    stores = []
    for first in range(0, HALF, T_STEP):
        rows = table_ref[pl.ds(0, T_STEP)]
        if first > 0:
            column = lax.broadcasted_iota(jnp.int32, rows.shape, 1)
            rows = jnp.where(column % 2 == 0, rows.astype(jnp.float32), -rows.astype(jnp.float32)).astype(jnp.bfloat16)
        even = jnp.dot(rows, sides[0], preferred_element_type=jnp.float32)
        rows = table_ref[pl.ds(T_STEP + first, T_STEP)]
        odd = jnp.dot(rows, sides[1], preferred_element_type=jnp.float32)
        if first == 0:
            load.wait()
            block_ref[:C, :C] = inverse_ref[...]
            block_ref[C:, C:] = inverse_ref[...]
            block = block_ref[...]
        for i in range(0, T_STEP, T_CHUNK):
            chunk = slice(i, i + T_CHUNK)
            for half, sums in enumerate((even[chunk] + odd[chunk], even[chunk] - odd[chunk])):
                where = pl.ds(half * HALF + first + i, T_CHUNK)
                for s in range(0, SD, 2):
                    update = [
                        high_ref[j, where].astype(jnp.float32) + low_ref[j, where].astype(jnp.float32)
                        for j in (s, s + 1)
                    ]
                    update = jnp.concatenate(update, axis=1)
                    reduced = (sums[:, s * C : (s + 2) * C] - update).astype(jnp.bfloat16)
                    both = jnp.dot(reduced, block, preferred_element_type=jnp.float32).astype(jnp.bfloat16)
                    out_ref[s, where] = both[:, :C]
                    out_ref[s + 1, where] = both[:, C:]
                copy = pltpu.make_async_copy(out_ref.at[:, where], out_hbm.at[:, where], sems.at[len(stores)])
                copy.start()
                stores.append(copy)
    for copy in stores:
        copy.wait()


def panel_rows(table, recv, high, low, inverse):
    return pl.pallas_call(
        panel_kernel,
        in_specs=[pl.BlockSpec(memory_space=pltpu.VMEM)] * 4 + [pl.BlockSpec(memory_space=pl.ANY)],
        out_specs=pl.BlockSpec(memory_space=pl.ANY),
        out_shape=jax.ShapeDtypeStruct((SD, NT, C), jnp.bfloat16),
        scratch_shapes=[
            pltpu.VMEM((SD, NT, C), jnp.bfloat16),
            pltpu.VMEM((C, C), jnp.bfloat16),
            pltpu.VMEM((2 * C, 2 * C), jnp.bfloat16),
            pltpu.SemaphoreType.DMA((NT // T_CHUNK,)),
            pltpu.SemaphoreType.DMA,
        ],
        compiler_params=pltpu.CompilerParams(vmem_limit_bytes=24 * 2**20),
        name="panel",
    )(table, recv, high, low, inverse)


def gather_pivots(pivot_store, owners):
    mine = jnp.repeat(owners == lax.axis_index("grp"), C)[None, :]
    value = jnp.where(mine, pivot_store, jnp.zeros_like(pivot_store))
    for bit in (1, 2, 4):
        value = value + lax.ppermute(value, "grp", [(g, g ^ bit) for g in range(N_GRP)])
    return value


def per_device(transfer, adjoint, lower_rows, pivot_store, owners, inverse_factor):
    rows = spectra_rows(transfer, adjoint)
    rows = rows.reshape(N_FREQ, SD, 2, KL, C)
    recv = lax.all_to_all(rows, "freq", split_axis=0, concat_axis=0, axis_index_groups=[ORDER], tiled=True)
    pivots = gather_pivots(pivot_store, owners)
    high, low = update_rows(lower_rows, pivots)
    out = panel_rows(jnp.asarray(table_parts()), recv, high.reshape(SD, NT, C), low.reshape(SD, NT, C), inverse_factor)
    return out.reshape(SD * NT, C)


def solution(mesh):
    in_specs = (
        P("freq", None, "grp", None),
        P("freq", None, None, None),
        P(("grp", "freq"), None),
        P("grp", None),
        P(),
        P(),
    )
    out_specs = P(("grp", "freq"), None)
    return jax.shard_map(
        per_device, mesh=mesh, in_specs=in_specs, out_specs=out_specs, check_vma=False
    )
```

```python
import math

import jax
import jax.numpy as jnp
import numpy as np
from jax import lax
from jax.experimental import pallas as pl
from jax.experimental.pallas import tpu as pltpu
from jax.sharding import PartitionSpec as P

C = 128
M = 512
NF = 512
PANELS = 3
NT = 1024
NS = 1024
N_GRP = 8
N_FREQ = 32
KL = NF // N_FREQ
SL = NS // N_GRP
SD = SL // N_FREQ
ORDER = [x * 16 + (z + 5 - x) % 8 * 2 + 1 - core for x in range(2) for z in range(8) for core in range(2)]
ROWS = 2 * KL
PITCH = ROWS + 1
LOADS = 4
HALF = NT // 2
T_STEP = HALF // 2
T_CHUNK = 128


def table_parts():
    phases = np.arange(HALF)[:, None] * np.arange(NF)[None, :] % NT * (2.0 * math.pi / NT)
    table = np.stack([np.cos(phases), -np.sin(phases)], axis=1) / math.sqrt(NF)
    table = table.reshape(HALF, 2, N_FREQ, KL // 2, 2)[:, :, ORDER].transpose(4, 0, 2, 1, 3).reshape(2, HALF, NF)
    return np.concatenate([table[0, : HALF // 2], table[1]]).astype(jnp.bfloat16)


def spectra_kernel(
    transfer_hbm, adjoint_hbm, out_hbm, transfer_ref, adjoint_ref, rows_ref, out_ref, load_sems, out_sems
):
    per = KL // 2 // LOADS
    loads = []
    for parity in range(2):
        for i in range(LOADS):
            part = pl.ds(i * per, per)
            for j, (src, dst) in enumerate(((transfer_hbm, transfer_ref), (adjoint_hbm, adjoint_ref))):
                copy = pltpu.make_async_copy(src.at[part, parity], dst.at[parity, part], load_sems.at[j, parity, i])
                copy.start()
                loads.append(copy)
    stores = []
    for parity in range(2):
        for k in range(KL // 2):
            if k % per == 0:
                first = 2 * (parity * LOADS + k // per)
                loads[first].wait()
                loads[first + 1].wait()
            left = transfer_ref[parity, k].reshape(2 * SL, M)
            right = jnp.concatenate([adjoint_ref[parity, k, 0], adjoint_ref[parity, k, 1]], axis=1)
            full = jnp.dot(left, right, preferred_element_type=jnp.float32)
            row = parity * KL + k
            rows_ref[pl.ds(row, SL, stride=PITCH), :] = full[:SL, :C] - full[SL:, C:]
            rows_ref[pl.ds(row + KL // 2, SL, stride=PITCH), :] = full[:SL, C:] + full[SL:, :C]
        for s in range(SL):
            place = ORDER.index(s // SD) * SD + s % SD
            out_ref[place, parity] = rows_ref[pl.ds(s * PITCH + parity * KL, KL), :].astype(jnp.bfloat16)
        copy = pltpu.make_async_copy(out_ref.at[:, parity], out_hbm.at[:, parity], out_sems.at[parity])
        copy.start()
        stores.append(copy)
    for copy in stores:
        copy.wait()


def spectra_rows(transfer, adjoint):
    return pl.pallas_call(
        spectra_kernel,
        in_specs=[pl.BlockSpec(memory_space=pl.ANY)] * 2,
        out_specs=pl.BlockSpec(memory_space=pl.ANY),
        out_shape=jax.ShapeDtypeStruct((SL, 2, KL, C), jnp.bfloat16),
        scratch_shapes=[
            pltpu.VMEM((2, KL // 2, 2, SL, M), jnp.bfloat16),
            pltpu.VMEM((2, KL // 2, 2, M, C), jnp.bfloat16),
            pltpu.VMEM((SL * PITCH + PITCH + 7, C), jnp.float32),
            pltpu.VMEM((SL, 2, KL, C), jnp.bfloat16),
            pltpu.SemaphoreType.DMA((2, 2, LOADS)),
            pltpu.SemaphoreType.DMA((2,)),
        ],
        compiler_params=pltpu.CompilerParams(vmem_limit_bytes=60 * 2**20),
        name="spectra",
    )(transfer.reshape(KL // 2, 2, 2, SL, M), adjoint.reshape(KL // 2, 2, 2, M, C))


def update_kernel(lower_ref, pivots_ref, high_ref, low_ref):
    update = lax.dot_general(
        lower_ref[...], pivots_ref[...], (((1,), (1,)), ((), ())), preferred_element_type=jnp.float32
    )
    high = update.astype(jnp.bfloat16)
    high_ref[...] = high
    low_ref[...] = (update - high.astype(jnp.float32)).astype(low_ref.dtype)


def update_rows(lower, pivots):
    rows = lower.shape[0]
    return pl.pallas_call(
        update_kernel,
        in_specs=[pl.BlockSpec(memory_space=pltpu.VMEM)] * 2,
        out_specs=[pl.BlockSpec(memory_space=pltpu.VMEM)] * 2,
        out_shape=[
            jax.ShapeDtypeStruct((rows, C), jnp.bfloat16),
            jax.ShapeDtypeStruct((rows, C), jnp.float8_e5m2),
        ],
        compiler_params=pltpu.CompilerParams(vmem_limit_bytes=24 * 2**20),
        cost_estimate=pl.CostEstimate(
            flops=2 * rows * PANELS * C * C, bytes_accessed=rows * (PANELS * C * 2 + C * 3), transcendentals=0
        ),
        name="update",
    )(lower, pivots)


def panel_kernel(
    table_ref, recv_ref, high_ref, low_ref, inverse_hbm, out_hbm, out_ref, inverse_ref, block_ref, sems, sem
):
    load = pltpu.make_async_copy(inverse_hbm, inverse_ref, sem)
    load.start()
    block_ref[...] = jnp.zeros_like(block_ref)
    sides = []
    for parity in range(2):
        cols = [recv_ref[:, s, parity].reshape(NF, C) for s in range(SD)]
        sides.append(jnp.concatenate(cols, axis=1))
    stores = []
    for first in range(0, HALF, T_STEP):
        rows = table_ref[pl.ds(0, T_STEP)]
        if first > 0:
            column = lax.broadcasted_iota(jnp.int32, rows.shape, 1)
            rows = jnp.where(column % 2 == 0, rows.astype(jnp.float32), -rows.astype(jnp.float32)).astype(jnp.bfloat16)
        even = jnp.dot(rows, sides[0], preferred_element_type=jnp.float32)
        rows = table_ref[pl.ds(T_STEP + first, T_STEP)]
        odd = jnp.dot(rows, sides[1], preferred_element_type=jnp.float32)
        if first == 0:
            load.wait()
            block_ref[:C, :C] = inverse_ref[...]
            block_ref[C:, C:] = inverse_ref[...]
            block = block_ref[...]
        for i in range(0, T_STEP, T_CHUNK):
            chunk = slice(i, i + T_CHUNK)
            for half, sums in enumerate((even[chunk] + odd[chunk], even[chunk] - odd[chunk])):
                where = pl.ds(half * HALF + first + i, T_CHUNK)
                for s in range(0, SD, 2):
                    update = [
                        high_ref[j, where].astype(jnp.float32) + low_ref[j, where].astype(jnp.float32)
                        for j in (s, s + 1)
                    ]
                    update = jnp.concatenate(update, axis=1)
                    reduced = (sums[:, s * C : (s + 2) * C] - update).astype(jnp.bfloat16)
                    both = jnp.dot(reduced, block, preferred_element_type=jnp.float32).astype(jnp.bfloat16)
                    out_ref[s, where] = both[:, :C]
                    out_ref[s + 1, where] = both[:, C:]
                copy = pltpu.make_async_copy(out_ref.at[:, where], out_hbm.at[:, where], sems.at[len(stores)])
                copy.start()
                stores.append(copy)
    for copy in stores:
        copy.wait()


def panel_rows(table, recv, high, low, inverse):
    return pl.pallas_call(
        panel_kernel,
        in_specs=[pl.BlockSpec(memory_space=pltpu.VMEM)] * 4 + [pl.BlockSpec(memory_space=pl.ANY)],
        out_specs=pl.BlockSpec(memory_space=pl.ANY),
        out_shape=jax.ShapeDtypeStruct((SD, NT, C), jnp.bfloat16),
        scratch_shapes=[
            pltpu.VMEM((SD, NT, C), jnp.bfloat16),
            pltpu.VMEM((C, C), jnp.bfloat16),
            pltpu.VMEM((2 * C, 2 * C), jnp.bfloat16),
            pltpu.SemaphoreType.DMA((NT // T_CHUNK,)),
            pltpu.SemaphoreType.DMA,
        ],
        compiler_params=pltpu.CompilerParams(vmem_limit_bytes=24 * 2**20),
        name="panel",
    )(table, recv, high, low, inverse)


def gather_pivots(pivot_store, owners):
    mine = jnp.repeat(owners == lax.axis_index("grp"), C)[None, :]
    value = jnp.where(mine, pivot_store, jnp.zeros_like(pivot_store))
    for bit in (1, 2, 4):
        value = value + lax.ppermute(value, "grp", [(g, g ^ bit) for g in range(N_GRP)])
    return value


def per_device(transfer, adjoint, lower_rows, pivot_store, owners, inverse_factor):
    rows = spectra_rows(transfer, adjoint)
    rows = rows.reshape(N_FREQ, SD, 2, KL, C)
    recv = lax.all_to_all(rows, "freq", split_axis=0, concat_axis=0, axis_index_groups=[ORDER], tiled=True)
    pivots = gather_pivots(pivot_store, owners)
    high, low = update_rows(lower_rows, pivots)
    out = panel_rows(jnp.asarray(table_parts()), recv, high.reshape(SD, NT, C), low.reshape(SD, NT, C), inverse_factor)
    return out.reshape(SD * NT, C)


def solution(mesh):
    in_specs = (
        P("freq", None, "grp", None),
        P("freq", None, None, None),
        P(("grp", "freq"), None),
        P("grp", None),
        P(),
        P(),
    )
    out_specs = P(("grp", "freq"), None)
    return jax.shard_map(
        per_device, mesh=mesh, in_specs=in_specs, out_specs=out_specs, check_vma=False
    )
```
